32 devices in a mesh: chan: 8 (over z, x), mode: 4 (over y, core).
Axes of the slice: x: 2, y: 2, z: 4, core: 2. Of those that a mesh axis runs over, the one named last changes fastest.
Arguments:
- weight: bfloat16 [512, 2, 32, 32, 256], P('chan', None, 'mode'), may hold values from -0.59765625 to 0.59765625
- gradient: bfloat16 [512, 2, 32, 32, 256], P('chan', None, 'mode'), may hold values from -6 to 6
- first_moment: float32 [128, 2, 16, 16, 128], P('chan', None, None, 'mode'), may hold values from -2 to 2
- second_moment: float32 [128, 2, 16, 16, 128], P('chan', None, None, 'mode'), may hold values from 0.0005 to 0.02
- u_in: float32 [512, 128], P('chan'), may hold values from -0.25 to 0.25
- u_out: bfloat16 [256, 128], replicated, may hold values from -0.375 to 0.375
- u_modes_a: float32 [32, 16], replicated, may hold values from -1 to 1
- u_modes_b: float32 [32, 16], replicated, may hold values from -1 to 1
Outputs:
- new_weight: bfloat16 [512, 2, 32, 32, 256], P('chan', None, 'mode')
- new_first: float32 [128, 2, 16, 16, 128], P('chan', None, None, 'mode')
- new_second: float32 [128, 2, 16, 16, 128], P('chan', None, None, 'mode')
The draws below stay inside these ranges and needn't reach their ends.
All inputs are finite; a program needn't handle non-finite values.
Results may differ from the reference program's by a relative error of at most 0.004.
Values sent between devices are 32-bit elements; how exact they have to be, the bound alone decides.
A program may use at most 128 MiB of HBM per device.

```python
import math
import jax
import jax.numpy as jnp
from jax import lax

IN_CH = 512
OUT_CH = 256
MODES_A = 32
MODES_B = 32
RANK_IN = 128
RANK_OUT = 128
RANK_A = 16
RANK_B = 16
STEP = 4


def levels(own_key, shape, cuts, low, largest):
    gain = 1.0
    for dim, shards_of in cuts:
        steps = jax.random.uniform(jax.random.fold_in(jax.random.fold_in(own_key, 6), dim), (shards_of,), jnp.float32, low / len(cuts), largest / len(cuts))
        gain = gain * jnp.repeat(jnp.exp(steps), shape[dim] // shards_of).reshape((-1,) + (1,) * (len(shape) - 1 - dim))
    return gain


def normal_values(key, shape, scale, most, shards=(), dtype=jnp.bfloat16):
    result = jax.random.normal(key, shape, jnp.float32) * scale
    if len(shards) > 0:
        result = levels(key, shape, shards, -0.22, 0.18) * result
    return jnp.clip(result, min=-most, max=most).astype(dtype)


def setup_inputs(seed: int = 0) -> dict:
    key_list = jax.random.split(jax.random.key(seed), 9)
    return {
        "weight": normal_values(key_list[0], (IN_CH, 2, MODES_A, MODES_B, OUT_CH), 0.1, 0.59765625, ((0, 8), (2, 4))),
        "gradient": normal_values(key_list[1], (IN_CH, 2, MODES_A, MODES_B, OUT_CH), 1.0, 6.0, ((0, 8), (2, 4))),
        "first_moment": normal_values(key_list[2], (RANK_IN, 2, RANK_A, RANK_B, RANK_OUT), 0.3, 2.0, ((0, 8), (3, 4)), jnp.float32),
        "second_moment": jnp.clip(jnp.exp(math.log(0.02) - 3.6888794 * jax.random.uniform(key_list[3], (RANK_IN, 2, RANK_A, RANK_B, RANK_OUT), jnp.float32) ** levels(key_list[3], (RANK_IN, 2, RANK_A, RANK_B, RANK_OUT), ((0, 8), (3, 4)), -0.2, 0.2)), 0.0005, 0.02),
        "u_in": normal_values(key_list[4], (IN_CH, RANK_IN), IN_CH ** -0.5, 0.25, ((0, 8),), jnp.float32),
        "u_out": normal_values(key_list[5], (OUT_CH, RANK_OUT), OUT_CH ** -0.5, 0.375),
        "u_modes_a": normal_values(key_list[6], (MODES_A, RANK_A), MODES_A ** -0.5, 1.0, (), jnp.float32),
        "u_modes_b": normal_values(key_list[7], (MODES_B, RANK_B), MODES_B ** -0.5, 1.0, (), jnp.float32),
    }


HIGH = lax.Precision.HIGHEST
beta_one = 0.9
beta_two = 0.999
step_rate = 0.5

def reference(weight, gradient, first_moment, second_moment, u_in, u_out, u_modes_a, u_modes_b):
    rows = math.gcd(IN_CH, 64)
    nblocks = IN_CH // rows
    grad_blocks = gradient.reshape(nblocks, rows, 2, MODES_A, MODES_B, OUT_CH)
    weight_blocks = weight.reshape(nblocks, rows, 2, MODES_A, MODES_B, OUT_CH)
    factor_blocks = u_in.reshape(nblocks, rows, RANK_IN)

    def project(carry, pair):
        block, factor = pair
        reduced = jnp.dot(block.reshape(-1, OUT_CH), u_out, preferred_element_type=jnp.float32)
        reduced = reduced.reshape(rows, 2, MODES_A, MODES_B, RANK_OUT)
        narrowed = jnp.einsum('ipabo,bs->ipaso', reduced, u_modes_b, precision=HIGH)
        mixed = jnp.einsum('ipaso,ar->iprso', narrowed, u_modes_a, precision=HIGH)
        return (carry + jnp.einsum('ik,iprso->kprso', factor, mixed, precision=HIGH), None)
    start = jnp.zeros((RANK_IN, 2, RANK_A, RANK_B, RANK_OUT), jnp.float32)
    core, unused = lax.scan(project, start, (grad_blocks, factor_blocks))
    new_first = beta_one * first_moment + (1.0 - beta_one) * core
    new_second = beta_two * second_moment + (1.0 - beta_two) * core * core
    direction = new_first / (1.0 - beta_one ** STEP) / (jnp.sqrt(new_second / (1.0 - beta_two ** STEP)) + 1e-08)

    def restore(pair):
        block, factor = pair
        spread = jnp.einsum('ik,kprso->iprso', factor, direction, precision=HIGH)
        wide = jnp.einsum('iprso,ar->ipaso', spread, u_modes_a, precision=HIGH)
        expanded = jnp.einsum('ipaso,bs->ipabo', wide, u_modes_b, precision=HIGH).astype(jnp.bfloat16)
        update = jnp.dot(expanded.reshape(-1, RANK_OUT), u_out.T, preferred_element_type=jnp.float32)
        update = update.reshape(rows, 2, MODES_A, MODES_B, OUT_CH)
        return (block.astype(jnp.float32) - step_rate * update).astype(jnp.bfloat16)
    new_weight = lax.map(restore, (weight_blocks, factor_blocks)).reshape(weight.shape)
    return (new_weight, new_first, new_second)
```

```python
import functools

import jax
import jax.numpy as jnp
from jax import lax
from jax.experimental import pallas as pl
from jax.experimental.pallas import tpu as pltpu
from jax.sharding import PartitionSpec as P

STEP = 4
BETA_ONE = 0.9
BETA_TWO = 0.999
STEP_RATE = 0.5
F32 = jnp.float32
BF16 = jnp.bfloat16
ROWS = 8
GROUPS = 2


def split(value):
    high = value.astype(BF16)
    return high, (value - high.astype(F32)).astype(BF16)


def dot(left, right):
    return jnp.dot(left, right, preferred_element_type=F32)


def dot3(left, right):
    left_high, left_low = left
    right_high, right_low = split(right)
    return dot(left_high, right_high) + (dot(left_high, right_low) + dot(left_low, right_high))


def turn(value, start):
    twice = jnp.concatenate([value, value])
    return lax.dynamic_slice_in_dim(twice, start, value.shape[0], 0)


def turn_back(value, start):
    return turn(value[::-1], value.shape[0] - 1 - start)


def call(body, grid, in_specs, out_specs, out_shape, scratch, flops, size):
    return pl.pallas_call(
        body,
        grid=grid,
        in_specs=in_specs,
        out_specs=out_specs,
        out_shape=out_shape,
        scratch_shapes=scratch,
        compiler_params=pltpu.CompilerParams(vmem_limit_bytes=40 * 1024 * 1024),
        cost_estimate=pl.CostEstimate(flops=flops, bytes_accessed=size, transcendentals=0),
    )


def narrow(gradient, u_out, select, part, modes, groups):
    ins, _, local_a, modes_b, out_ch = gradient.shape
    rank_out = u_out.shape[1]
    ranks = select.shape[0] // (ROWS * modes)
    each = ranks // groups

    def body(grad_ref, factor_ref, select_ref, *outs):
        matrix = split(select_ref[...])
        factor = factor_ref[...]
        for block in range(ins // ROWS):
            rows = pl.ds(block * ROWS, ROWS)
            lines = grad_ref[rows, 0, 0].reshape(ROWS * modes_b, out_ch)
            done = dot3(matrix, dot(lines, factor)).reshape(modes, groups, each, ROWS, rank_out)
            for peer in range(modes):
                for group in range(groups):
                    outs[peer * groups + group][0, :, rows, :] = done[peer, group]

    count = modes * groups
    spec = pl.BlockSpec((1, each, ins, rank_out), lambda a: (a, 0, 0, 0))
    shape = jax.ShapeDtypeStruct((local_a, each, ins, rank_out), F32)
    return call(
        body,
        (local_a,),
        [
            pl.BlockSpec((ins, 1, 1, modes_b, out_ch), lambda a: (0, part, a, 0, 0)),
            pl.BlockSpec(u_out.shape, lambda a: (0, 0)),
            pl.BlockSpec(select.shape, lambda a: (0, 0)),
        ],
        [spec] * count,
        [shape] * count,
        [],
        2 * ins * local_a * modes_b * out_ch * rank_out * 4,
        ins * local_a * modes_b * out_ch * 3,
    )(gradient, u_out, select)


def gather_core(pieces, select, columns, rank_a, across, along):
    modes = len(pieces)
    local_a, each, ins, rank_out = pieces[0].shape
    rank_in = columns.shape[0]
    own = rank_in // (across * along)

    def body(*refs):
        xs, select_ref, columns_ref = refs[:modes], refs[modes], refs[modes + 1]
        outs, mixed = refs[modes + 2 : -1], refs[-1]
        matrix = split(select_ref[...])
        for block in range(ins // ROWS):
            rows = pl.ds(block * ROWS, ROWS)
            lines = jnp.concatenate(
                [x[:, 0, rows, :].reshape(local_a * ROWS, rank_out) for x in xs], axis=0
            )
            done = dot3(matrix, lines)
            for r in range(rank_a):
                mixed[rows, r * rank_out : (r + 1) * rank_out] = done[r * ROWS : (r + 1) * ROWS]
        left = split(columns_ref[...])
        for r in range(rank_a):
            done = dot3(left, mixed[:, r * rank_out : (r + 1) * rank_out])
            done = done.reshape(across, along, own, rank_out)
            for x in range(across):
                outs[x][:, r, 0] = done[x]

    return call(
        body,
        (each,),
        [pl.BlockSpec((local_a, 1, ins, rank_out), lambda s: (0, s, 0, 0))] * modes
        + [pl.BlockSpec(select.shape, lambda s: (0, 0)), pl.BlockSpec(columns.shape, lambda s: (0, 0))],
        [pl.BlockSpec((along, rank_a, 1, own, rank_out), lambda s: (0, 0, s, 0, 0))] * across,
        [jax.ShapeDtypeStruct((along, rank_a, each, own, rank_out), F32)] * across,
        [pltpu.VMEM((ins, rank_a * rank_out), F32)],
        2 * each * rank_a * ins * rank_in * rank_out * 6,
        4 * each * rank_out * (modes * local_a * ins + rank_in * rank_a),
    )(*pieces, select, columns)


def spread_back(pieces, select, columns, modes):
    across = len(pieces)
    along, rank_a, each, own, rank_out = pieces[0].shape
    ins = columns.shape[0]
    local_a = select.shape[0] // (ROWS * modes)

    def body(*refs):
        xs, select_ref, columns_ref = refs[:across], refs[across], refs[across + 1]
        outs, spread = refs[across + 2 : -1], refs[-1]
        left = split(columns_ref[...])
        for r in range(rank_a):
            lines = jnp.concatenate(
                [x[:, r, 0].reshape(along * own, rank_out) for x in xs], axis=0
            )
            spread[r] = dot3(left, lines)
        matrix = split(select_ref[...])
        for block in range(ins // ROWS):
            rows = pl.ds(block * ROWS, ROWS)
            done = dot3(matrix, spread[:, rows, :].reshape(rank_a * ROWS, rank_out))
            done = done.reshape(modes, local_a, ROWS, rank_out)
            for peer in range(modes):
                outs[peer][:, 0, rows, :] = done[peer]

    return call(
        body,
        (each,),
        [pl.BlockSpec((along, rank_a, 1, own, rank_out), lambda s: (0, 0, s, 0, 0))] * across
        + [pl.BlockSpec(select.shape, lambda s: (0, 0)), pl.BlockSpec(columns.shape, lambda s: (0, 0))],
        [pl.BlockSpec((local_a, 1, ins, rank_out), lambda s: (0, s, 0, 0))] * modes,
        [jax.ShapeDtypeStruct((local_a, each, ins, rank_out), F32)] * modes,
        [pltpu.VMEM((rank_a, ins, rank_out), F32)],
        2 * each * rank_a * ins * columns.shape[1] * rank_out * 6,
        4 * each * rank_out * (modes * local_a * ins + columns.shape[1] * rank_a),
    )(*pieces, select, columns)


def update(weight, pieces, back, select, previous, part, groups):
    ins, _, local_a, modes_b, out_ch = weight.shape
    count = len(pieces)
    each, rank_out = pieces[0].shape[1], pieces[0].shape[3]
    extra = [] if previous is None else [previous]

    def body(weight_ref, *refs):
        xs, back_ref, select_ref, out_ref = refs[:count], refs[count], refs[count + 1], refs[-1]
        matrix = split(select_ref[...])
        factor = back_ref[...]
        for block in range(ins // ROWS):
            rows = pl.ds(block * ROWS, ROWS)
            lines = jnp.concatenate(
                [x[0, :, rows, :].reshape(each * ROWS, rank_out) for x in xs], axis=0
            )
            expanded = dot3(matrix, lines).astype(BF16)
            change = dot(expanded, factor).reshape(ROWS, modes_b, out_ch)
            old = weight_ref[rows, 0, 0].astype(F32)
            out_ref[rows, 0, 0] = (old - STEP_RATE * change).astype(BF16)

    spec = pl.BlockSpec((ins, 1, 1, modes_b, out_ch), lambda a: (0, part, a, 0, 0))
    return pl.pallas_call(
        body,
        grid=(local_a,),
        in_specs=[spec]
        + [pl.BlockSpec((1, each, ins, rank_out), lambda a: (a, 0, 0, 0))] * count
        + [pl.BlockSpec(back.shape, lambda a: (0, 0)), pl.BlockSpec(select.shape, lambda a: (0, 0))]
        + [pl.BlockSpec(memory_space=pl.ANY)] * len(extra),
        out_specs=spec,
        out_shape=jax.ShapeDtypeStruct(weight.shape, BF16),
        input_output_aliases={} if previous is None else {count + 3: 0},
        compiler_params=pltpu.CompilerParams(vmem_limit_bytes=40 * 1024 * 1024),
        cost_estimate=pl.CostEstimate(
            flops=2 * ins * local_a * modes_b * out_ch * rank_out * 4,
            bytes_accessed=ins * local_a * modes_b * out_ch * 5,
            transcendentals=0,
        ),
    )(weight, *pieces, back, select, *extra)


def shards(chan, modes, weight, gradient, first_moment, second_moment, u_in, u_out, u_modes_a, u_modes_b):
    ins, parts, local_a, modes_b, out_ch = gradient.shape
    own, _, rank_a, ranks, rank_out = first_moment.shape
    groups = GROUPS if ranks % GROUPS == 0 else 1
    across = max(d for d in range(1, chan + 1) if chan % d == 0 and d * d <= chan)
    along = chan // across
    here = lax.axis_index("chan")
    mode = lax.axis_index("mode")
    z, x = here // across, here % across
    eye = jnp.eye(ROWS, dtype=F32)

    factor_b = u_modes_b.T.reshape(modes, groups, ranks // groups, modes_b)
    factor_a = u_modes_a.reshape(modes, local_a, rank_a)
    narrow_b = jnp.einsum("dgsb,ij->dgsijb", turn(factor_b, mode), eye, precision="highest")
    narrow_b = narrow_b.reshape(modes * ranks * ROWS, ROWS * modes_b)
    widen_b = jnp.einsum("dgsb,ij->jbdgsi", turn_back(factor_b, mode), eye, precision="highest")
    widen_b = widen_b.reshape(ROWS * modes_b, modes * ranks * ROWS)
    narrow_a = jnp.einsum("dar,ij->ridaj", turn_back(factor_a, mode), eye, precision="highest")
    narrow_a = narrow_a.reshape(rank_a * ROWS, modes * local_a * ROWS)
    widen_a = jnp.einsum("dar,ij->dairj", turn(factor_a, mode), eye, precision="highest")
    widen_a = widen_a.reshape(modes * local_a * ROWS, rank_a * ROWS)

    columns = u_in.reshape(ins, along, across, own).transpose(2, 1, 3, 0)
    forward_columns = turn(columns, x).reshape(-1, ins)
    turned = turn(turn_back(columns, x).transpose(1, 0, 2, 3), z).transpose(1, 0, 2, 3)
    backward_columns = turned.reshape(-1, ins).T

    def to_mode(value, d):
        if d == 0:
            return value
        return lax.ppermute(value, "mode", [(m, (m + d) % modes) for m in range(modes)])

    def to_across(value, d):
        pairs = [
            (q * across + c, q * across + (c + d) % across)
            for q in range(along)
            for c in range(across)
        ]
        return lax.ppermute(value, "chan", pairs)

    def to_along(value, sign, sources):
        pairs = [
            (q * across + c, (q + sign) * across + c) for q in sources for c in range(across)
        ]
        return lax.ppermute(value, "chan", pairs)

    def scatter(held):
        arrived = [held[0]] + [to_across(held[d], d) for d in range(1, across)]

        def local(q):
            q = jnp.clip(q, 0, along - 1)
            terms = [lax.dynamic_index_in_dim(v, q, 0, keepdims=False) for v in arrived]
            return functools.reduce(jnp.add, terms)

        right = left = None
        last = along - 1
        for t in range(last):
            send_right, send_left = local(last - t + z), local(t - last + z)
            if t > 0:
                send_right, send_left = send_right + right, send_left + left
            right = to_along(send_right, 1, range(t + 1))
            left = to_along(send_left, -1, range(last - t, along))
        total = local(z)
        return total if last == 0 else total + right + left

    def gather(value):
        last = along - 1
        rights, lefts = [], []
        right = left = value
        for t in range(last):
            right = to_along(right, 1, range(t, last))
            left = to_along(left, -1, range(1, along - t))
            rights.append(right)
            lefts.append(left)
        slots = [value] + [lefts[j - 1] + rights[last - j] for j in range(1, along)]
        full = jnp.stack(slots)
        return [full] + [to_across(full, d) for d in range(1, across)]

    shares = {}
    for p in range(parts):
        narrowed = narrow(gradient, u_out, narrow_b, p, modes, groups)
        for g in range(groups):
            pieces = [to_mode(narrowed[d * groups + g], d) for d in range(modes)]
            held = gather_core(pieces, narrow_a, forward_columns, rank_a, across, along)
            shares[p, g] = scatter(held)

    wides, firsts, seconds = {}, [], []
    each = ranks // groups
    for p in range(parts):
        first_parts, second_parts = [], []
        for g in range(groups):
            core = shares[p, g].transpose(2, 0, 1, 3)
            old_first = first_moment[:, p, :, g * each : (g + 1) * each]
            old_second = second_moment[:, p, :, g * each : (g + 1) * each]
            new_first = BETA_ONE * old_first + (1.0 - BETA_ONE) * core
            new_second = BETA_TWO * old_second + (1.0 - BETA_TWO) * core * core
            direction = (
                new_first
                / (1.0 - BETA_ONE**STEP)
                / (jnp.sqrt(new_second / (1.0 - BETA_TWO**STEP)) + 1e-08)
            )
            first_parts.append(new_first)
            second_parts.append(new_second)
            pieces = gather(direction.transpose(1, 2, 0, 3))
            outs = spread_back(pieces, widen_a, backward_columns, modes)
            for d in range(modes):
                wides[p, d, g] = to_mode(outs[d], d)
        firsts.append(jnp.concatenate(first_parts, axis=2))
        seconds.append(jnp.concatenate(second_parts, axis=2))

    new_weight = None
    back = u_out.T
    for p in range(parts):
        pieces = [wides[p, d, g] for d in range(modes) for g in range(groups)]
        new_weight = update(weight, pieces, back, widen_b, new_weight, p, groups)
    return (new_weight, jnp.stack(firsts, axis=1), jnp.stack(seconds, axis=1))


def solution(mesh):
    wide = P("chan", None, "mode", None, None)
    core = P("chan", None, None, "mode", None)
    body = functools.partial(shards, mesh.shape["chan"], mesh.shape["mode"])
    return jax.shard_map(
        body,
        mesh=mesh,
        in_specs=(wide, wide, core, core, P("chan", None), P(), P(), P()),
        out_specs=(wide, core, core),
        check_vma=False,
    )
```

```python
import functools

import jax
import jax.numpy as jnp
from jax import lax
from jax.experimental import pallas as pl
from jax.experimental.pallas import tpu as pltpu
from jax.sharding import PartitionSpec as P

STEP = 4
BETA_ONE = 0.9
BETA_TWO = 0.999
STEP_RATE = 0.5
F32 = jnp.float32
BF16 = jnp.bfloat16
ROWS = 8
GROUPS = 2


def split(value):
    high = value.astype(BF16)
    return high, (value - high.astype(F32)).astype(BF16)


def dot(left, right):
    return jnp.dot(left, right, preferred_element_type=F32)


def dot3(left, right):
    left_high, left_low = left
    right_high, right_low = split(right)
    return dot(left_high, right_high) + (dot(left_high, right_low) + dot(left_low, right_high))


def turn(value, start):
    twice = jnp.concatenate([value, value])
    return lax.dynamic_slice_in_dim(twice, start, value.shape[0], 0)


def turn_back(value, start):
    return turn(value[::-1], value.shape[0] - 1 - start)


def call(body, grid, in_specs, out_specs, out_shape, scratch, flops, size):
    return pl.pallas_call(
        body,
        grid=grid,
        in_specs=in_specs,
        out_specs=out_specs,
        out_shape=out_shape,
        scratch_shapes=scratch,
        compiler_params=pltpu.CompilerParams(vmem_limit_bytes=40 * 1024 * 1024),
        cost_estimate=pl.CostEstimate(flops=flops, bytes_accessed=size, transcendentals=0),
    )


def narrow(gradient, u_out, select, part, modes, groups):
    ins, _, local_a, modes_b, out_ch = gradient.shape
    rank_out = u_out.shape[1]
    ranks = select.shape[0] // (ROWS * modes)
    each = ranks // groups

    def body(grad_ref, factor_ref, select_ref, *outs):
        matrix = jnp.concatenate(split(select_ref[...]), axis=0)
        count = select_ref.shape[0]
        factor = factor_ref[...]
        for block in range(ins // ROWS):
            rows = pl.ds(block * ROWS, ROWS)
            lines = grad_ref[rows, 0, 0].reshape(ROWS * modes_b, out_ch)
            both = dot(matrix, lines)
            both = dot(jnp.concatenate(split(both[:count] + both[count:]), axis=0), factor)
            done = (both[:count] + both[count:]).reshape(modes, groups, each, ROWS, rank_out)
            for peer in range(modes):
                for group in range(groups):
                    outs[peer * groups + group][0, :, rows, :] = done[peer, group]

    count = modes * groups
    spec = pl.BlockSpec((1, each, ins, rank_out), lambda a: (a, 0, 0, 0))
    shape = jax.ShapeDtypeStruct((local_a, each, ins, rank_out), F32)
    return call(
        body,
        (local_a,),
        [
            pl.BlockSpec((ins, 1, 1, modes_b, out_ch), lambda a: (0, part, a, 0, 0)),
            pl.BlockSpec(u_out.shape, lambda a: (0, 0)),
            pl.BlockSpec(select.shape, lambda a: (0, 0)),
        ],
        [spec] * count,
        [shape] * count,
        [],
        2 * ins * local_a * modes_b * out_ch * rank_out * 4,
        ins * local_a * modes_b * out_ch * 3,
    )(gradient, u_out, select)


def gather_core(pieces, select, columns, rank_a, across, along):
    modes = len(pieces)
    local_a, each, ins, rank_out = pieces[0].shape
    rank_in = columns.shape[0]
    own = rank_in // (across * along)

    def body(*refs):
        xs, select_ref, columns_ref = refs[:modes], refs[modes], refs[modes + 1]
        outs, mixed = refs[modes + 2 : -1], refs[-1]
        matrix = split(select_ref[...])
        for block in range(ins // ROWS):
            rows = pl.ds(block * ROWS, ROWS)
            lines = jnp.concatenate(
                [x[:, 0, rows, :].reshape(local_a * ROWS, rank_out) for x in xs], axis=0
            )
            done = dot3(matrix, lines)
            for r in range(rank_a):
                mixed[rows, r * rank_out : (r + 1) * rank_out] = done[r * ROWS : (r + 1) * ROWS]
        left = split(columns_ref[...])
        for r in range(rank_a):
            done = dot3(left, mixed[:, r * rank_out : (r + 1) * rank_out])
            done = done.reshape(across, along, own, rank_out)
            for x in range(across):
                outs[x][:, r, 0] = done[x]

    return call(
        body,
        (each,),
        [pl.BlockSpec((local_a, 1, ins, rank_out), lambda s: (0, s, 0, 0))] * modes
        + [pl.BlockSpec(select.shape, lambda s: (0, 0)), pl.BlockSpec(columns.shape, lambda s: (0, 0))],
        [pl.BlockSpec((along, rank_a, 1, own, rank_out), lambda s: (0, 0, s, 0, 0))] * across,
        [jax.ShapeDtypeStruct((along, rank_a, each, own, rank_out), F32)] * across,
        [pltpu.VMEM((ins, rank_a * rank_out), F32)],
        2 * each * rank_a * ins * rank_in * rank_out * 6,
        4 * each * rank_out * (modes * local_a * ins + rank_in * rank_a),
    )(*pieces, select, columns)


def spread_back(pieces, select, columns, modes):
    across = len(pieces)
    along, rank_a, each, own, rank_out = pieces[0].shape
    ins = columns.shape[0]
    local_a = select.shape[0] // (ROWS * modes)

    def body(*refs):
        xs, select_ref, columns_ref = refs[:across], refs[across], refs[across + 1]
        outs, spread = refs[across + 2 : -1], refs[-1]
        left = split(columns_ref[...])
        for r in range(rank_a):
            lines = jnp.concatenate(
                [x[:, r, 0].reshape(along * own, rank_out) for x in xs], axis=0
            )
            spread[r] = dot3(left, lines)
        matrix = split(select_ref[...])
        for block in range(ins // ROWS):
            rows = pl.ds(block * ROWS, ROWS)
            done = dot3(matrix, spread[:, rows, :].reshape(rank_a * ROWS, rank_out))
            done = done.reshape(modes, local_a, ROWS, rank_out)
            for peer in range(modes):
                outs[peer][:, 0, rows, :] = done[peer]

    return call(
        body,
        (each,),
        [pl.BlockSpec((along, rank_a, 1, own, rank_out), lambda s: (0, 0, s, 0, 0))] * across
        + [pl.BlockSpec(select.shape, lambda s: (0, 0)), pl.BlockSpec(columns.shape, lambda s: (0, 0))],
        [pl.BlockSpec((local_a, 1, ins, rank_out), lambda s: (0, s, 0, 0))] * modes,
        [jax.ShapeDtypeStruct((local_a, each, ins, rank_out), F32)] * modes,
        [pltpu.VMEM((rank_a, ins, rank_out), F32)],
        2 * each * rank_a * ins * columns.shape[1] * rank_out * 6,
        4 * each * rank_out * (modes * local_a * ins + columns.shape[1] * rank_a),
    )(*pieces, select, columns)


def update(weight, pieces, back, select, previous, part, groups):
    ins, _, local_a, modes_b, out_ch = weight.shape
    count = len(pieces)
    each, rank_out = pieces[0].shape[1], pieces[0].shape[3]
    extra = [] if previous is None else [previous]

    def body(weight_ref, *refs):
        xs, back_ref, select_ref, out_ref = refs[:count], refs[count], refs[count + 1], refs[-1]
        matrix = split(select_ref[...])
        factor = back_ref[...]
        for block in range(ins // ROWS):
            rows = pl.ds(block * ROWS, ROWS)
            lines = jnp.concatenate(
                [x[0, :, rows, :].reshape(each * ROWS, rank_out) for x in xs], axis=0
            )
            expanded = dot3(matrix, lines).astype(BF16)
            change = dot(expanded, factor).reshape(ROWS, modes_b, out_ch)
            old = weight_ref[rows, 0, 0].astype(F32)
            out_ref[rows, 0, 0] = (old - STEP_RATE * change).astype(BF16)

    spec = pl.BlockSpec((ins, 1, 1, modes_b, out_ch), lambda a: (0, part, a, 0, 0))
    return pl.pallas_call(
        body,
        grid=(local_a,),
        in_specs=[spec]
        + [pl.BlockSpec((1, each, ins, rank_out), lambda a: (a, 0, 0, 0))] * count
        + [pl.BlockSpec(back.shape, lambda a: (0, 0)), pl.BlockSpec(select.shape, lambda a: (0, 0))]
        + [pl.BlockSpec(memory_space=pl.ANY)] * len(extra),
        out_specs=spec,
        out_shape=jax.ShapeDtypeStruct(weight.shape, BF16),
        input_output_aliases={} if previous is None else {count + 3: 0},
        compiler_params=pltpu.CompilerParams(vmem_limit_bytes=40 * 1024 * 1024),
        cost_estimate=pl.CostEstimate(
            flops=2 * ins * local_a * modes_b * out_ch * rank_out * 4,
            bytes_accessed=ins * local_a * modes_b * out_ch * 5,
            transcendentals=0,
        ),
    )(weight, *pieces, back, select, *extra)


def shards(chan, modes, weight, gradient, first_moment, second_moment, u_in, u_out, u_modes_a, u_modes_b):
    ins, parts, local_a, modes_b, out_ch = gradient.shape
    own, _, rank_a, ranks, rank_out = first_moment.shape
    groups = GROUPS if ranks % GROUPS == 0 else 1
    across = max(d for d in range(1, chan + 1) if chan % d == 0 and d * d <= chan)
    along = chan // across
    here = lax.axis_index("chan")
    mode = lax.axis_index("mode")
    z, x = here // across, here % across
    eye = jnp.eye(ROWS, dtype=F32)

    factor_b = u_modes_b.T.reshape(modes, groups, ranks // groups, modes_b)
    factor_a = u_modes_a.reshape(modes, local_a, rank_a)
    narrow_b = jnp.einsum("dgsb,ij->dgsijb", turn(factor_b, mode), eye, precision="highest")
    narrow_b = narrow_b.reshape(modes * ranks * ROWS, ROWS * modes_b)
    widen_b = jnp.einsum("dgsb,ij->jbdgsi", turn_back(factor_b, mode), eye, precision="highest")
    widen_b = widen_b.reshape(ROWS * modes_b, modes * ranks * ROWS)
    narrow_a = jnp.einsum("dar,ij->ridaj", turn_back(factor_a, mode), eye, precision="highest")
    narrow_a = narrow_a.reshape(rank_a * ROWS, modes * local_a * ROWS)
    widen_a = jnp.einsum("dar,ij->dairj", turn(factor_a, mode), eye, precision="highest")
    widen_a = widen_a.reshape(modes * local_a * ROWS, rank_a * ROWS)

    columns = u_in.reshape(ins, along, across, own).transpose(2, 1, 3, 0)
    forward_columns = turn(columns, x).reshape(-1, ins)
    turned = turn(turn_back(columns, x).transpose(1, 0, 2, 3), z).transpose(1, 0, 2, 3)
    backward_columns = turned.reshape(-1, ins).T

    def to_mode(value, d):
        if d == 0:
            return value
        return lax.ppermute(value, "mode", [(m, (m + d) % modes) for m in range(modes)])

    def to_across(value, d):
        pairs = [
            (q * across + c, q * across + (c + d) % across)
            for q in range(along)
            for c in range(across)
        ]
        return lax.ppermute(value, "chan", pairs)

    def to_along(value, sign, sources):
        pairs = [
            (q * across + c, (q + sign) * across + c) for q in sources for c in range(across)
        ]
        return lax.ppermute(value, "chan", pairs)

    def scatter(arrived):
        def local(q):
            q = jnp.clip(q, 0, along - 1)
            terms = [lax.dynamic_index_in_dim(v, q, 0, keepdims=False) for v in arrived]
            return functools.reduce(jnp.add, terms)

        right = left = None
        last = along - 1
        for t in range(last):
            send_right, send_left = local(last - t + z), local(t - last + z)
            if t > 0:
                send_right, send_left = send_right + right, send_left + left
            right = to_along(send_right, 1, range(t + 1))
            left = to_along(send_left, -1, range(last - t, along))
        total = local(z)
        return total if last == 0 else total + right + left

    def gather(value):
        last = along - 1
        rights, lefts = [], []
        right = left = value
        for t in range(last):
            right = to_along(right, 1, range(t, last))
            left = to_along(left, -1, range(1, along - t))
            rights.append(right)
            lefts.append(left)
        slots = [value] + [lefts[j - 1] + rights[last - j] for j in range(1, along)]
        return jnp.stack(slots)

    each = ranks // groups
    chunks = [(p, g) for p in range(parts) for g in range(groups)]
    narrowed = {}
    for p in range(parts):
        chosen = narrow_b
        if p > 0:
            chosen = lax.optimization_barrier((narrow_b, narrowed[p - 1]))[0]
        narrowed[p] = narrow(gradient, u_out, chosen, p, modes, groups)
    moments = {}

    def send_narrowed(key, pieces):
        return [to_mode(v, d) for d, v in enumerate(pieces)]

    def send_across(key, pieces):
        held = gather_core(pieces, narrow_a, forward_columns, rank_a, across, along)
        return [held[0]] + [to_across(held[d], d) for d in range(1, across)]

    def sum_along(key, arrived):
        return [scatter(arrived)]

    def step(key, state):
        p, g = key
        core = state[0].transpose(2, 0, 1, 3)
        old_first = first_moment[:, p, :, g * each : (g + 1) * each]
        old_second = second_moment[:, p, :, g * each : (g + 1) * each]
        new_first = BETA_ONE * old_first + (1.0 - BETA_ONE) * core
        new_second = BETA_TWO * old_second + (1.0 - BETA_TWO) * core * core
        direction = (
            new_first
            / (1.0 - BETA_ONE**STEP)
            / (jnp.sqrt(new_second / (1.0 - BETA_TWO**STEP)) + 1e-08)
        )
        moments[key] = (new_first, new_second)
        return [gather(direction.transpose(1, 2, 0, 3))]

    def share_across(key, state):
        return state + [to_across(state[0], d) for d in range(1, across)]

    def send_wide(key, pieces):
        outs = spread_back(pieces, widen_a, backward_columns, modes)
        return [to_mode(v, d) for d, v in enumerate(outs)]

    stages = [send_narrowed, send_across, sum_along, step, share_across, send_wide]
    states = [[narrowed[p][d * groups + g] for d in range(modes)] for p, g in chunks]
    for tick in range(len(chunks) + len(stages) - 1):
        active = [c for c in range(len(chunks)) if 0 <= tick - c < len(stages)]
        for c in active:
            states[c] = stages[tick - c](chunks[c], states[c])
        if tick + 1 < len(chunks):
            active = active + [tick + 1]
        held = lax.optimization_barrier([states[c] for c in active])
        for c, value in zip(active, held):
            states[c] = value
    wides = {(*chunks[c], d): states[c][d] for c in range(len(chunks)) for d in range(modes)}
    firsts, seconds = (
        [jnp.concatenate([moments[p, g][m] for g in range(groups)], axis=2) for p in range(parts)]
        for m in range(2)
    )

    new_weight = None
    back = u_out.T
    for p in range(parts):
        pieces = [wides[p, g, d] for d in range(modes) for g in range(groups)]
        new_weight = update(weight, pieces, back, widen_b, new_weight, p, groups)
    return (new_weight, jnp.stack(firsts, axis=1), jnp.stack(seconds, axis=1))


def solution(mesh):
    wide = P("chan", None, "mode", None, None)
    core = P("chan", None, None, "mode", None)
    body = functools.partial(shards, mesh.shape["chan"], mesh.shape["mode"])
    return jax.shard_map(
        body,
        mesh=mesh,
        in_specs=(wide, wide, core, core, P("chan", None), P(), P(), P()),
        out_specs=(wide, core, core),
        check_vma=False,
    )
```
